512 devices in a mesh: row: 16 (over y, x_lo, core), col: 32 (over x_hi, z).
Axes of the slice: x: 4 (x_hi: 2, x_lo: 2; x = x_hi * 2 + x_lo), y: 4, z: 16, core: 2. Of those that a mesh axis runs over, the one named last changes fastest.
Arguments:
- image_embed: bfloat16 [163840, 1152], P(('row', 'col')), as said below
- text_embed: bfloat16 [163840, 1152], P(('row', 'col')), as said below
Outputs:
- row_loss: float32 [163840], P(('row', 'col'))
- image_grad: float32 [163840, 1152], P(('row', 'col'))
- text_grad: float32 [163840, 1152], P(('row', 'col'))
Inputs may be any that keep to these rules, and one draw needn't show every extreme that they name: `image_embed`: no row is zero. `text_embed`: no row is zero.
All inputs are finite; a program needn't handle non-finite values.
Results may differ from the reference program's by a relative error of at most 0.0048.
Values may be sent and summed in bfloat16 or wider, within the bound.
No kernel may reach another device: no remote copies, remote signals or barrier semaphores. Data moves between devices by JAX's collectives and lax.ppermute only.
A program may use at most 64 MiB of HBM per device.

```python
import math
import jax
import jax.numpy as jnp
from jax import lax

D = 1152
B = 320
BATCH = 163840
N_ROW = 16
N_COL = 32


def row_scales(key, lowest, highest):
    spread = jax.random.uniform(key, (BATCH, 1), jnp.float32, math.log(lowest), math.log(highest))
    return jnp.exp(spread) / math.sqrt(D)


def draw_image_embed(key, part):
    key = jax.random.fold_in(key, 5)
    noise_key, scale_key = jax.random.split(key)
    row_scale = row_scales(scale_key, 0.3, 3.0)
    values = jnp.clip(jax.random.normal(noise_key, (BATCH, D), jnp.float32), -6.0, 6.0)
    return (values * row_scale).astype(jnp.bfloat16)


def draw_text_embed(key, part):
    key = jax.random.fold_in(key, 9)
    noise_key, scale_key = jax.random.split(key)
    row_scale = row_scales(scale_key, 0.3, 3.0)
    values = jnp.clip(jax.random.normal(noise_key, (BATCH, D), jnp.float32), -6.0, 6.0)
    return (values * row_scale).astype(jnp.bfloat16)


def setup_inputs(seed: int = 0) -> dict:
    streams_of = jax.random.split(jax.random.key(seed), 3)
    return {
        "image_embed": draw_image_embed(jax.random.fold_in(streams_of[2], 71), 0),
        "text_embed": draw_text_embed(jax.random.fold_in(streams_of[2], 71), 0),
    }


LOGIT_SCALE = 8.0
LOGIT_BIAS = -4.0
EPSILON = 1e-06
CONTRACT_ROWS = (((0,), (0,)), ((), ()))

def normalize_rows(raw_rows):
    widened = raw_rows.astype(jnp.float32)
    inverse = lax.rsqrt(lax.optimization_barrier(jnp.sum(widened * widened, axis=1, keepdims=True)) + EPSILON)
    return (widened * inverse, inverse)

def logit_block(left_rows, right_rows):
    product = lax.dot_general(left_rows, right_rows, (((1,), (1,)), ((), ())), preferred_element_type=jnp.float32)
    return LOGIT_SCALE * product + LOGIT_BIAS

def raw_gradient(normed, inverse, gradient):
    return inverse * (gradient - normed * lax.optimization_barrier(jnp.sum(normed * gradient, axis=1, keepdims=True)))

def reference(image_embed, text_embed):
    image_unit, image_inverse = normalize_rows(image_embed)
    text_unit, text_inverse = normalize_rows(text_embed)
    devices_all = N_ROW * N_COL
    image_blocks = image_unit.astype(jnp.bfloat16).reshape(devices_all, B, D)
    text_blocks = text_unit.astype(jnp.bfloat16).reshape(devices_all, B, D)
    offsets = (0, 1, 1 + N_COL, N_COL, N_COL + N_COL // 2, 1 + N_COL + N_COL // 2, 1 + N_COL // 2)
    identity = jnp.eye(B, dtype=jnp.float32)

    def per_device(device):
        own_image = lax.dynamic_index_in_dim(image_blocks, device, 0, keepdims=False)
        own_text = lax.dynamic_index_in_dim(text_blocks, device, 0, keepdims=False)
        row_losses = jnp.zeros((B,), jnp.float32)
        image_total = jnp.zeros((B, D), jnp.float32)
        text_total = jnp.zeros((B, D), jnp.float32)
        for offset in offsets:
            diagonal = identity if offset == 0 else jnp.zeros_like(identity)
            partner = jnp.bitwise_xor(device, jnp.int32(offset)).astype(jnp.int32)
            other_image = lax.dynamic_index_in_dim(image_blocks, partner, 0, keepdims=False)
            other_text = lax.dynamic_index_in_dim(text_blocks, partner, 0, keepdims=False)
            forward = logit_block(own_image, other_text)
            row_losses = row_losses + lax.optimization_barrier(jnp.sum(jnp.log1p(jnp.exp(forward)) - diagonal * forward, axis=1))
            weights = (jax.nn.sigmoid(forward) - diagonal).astype(jnp.bfloat16)
            image_total = image_total + LOGIT_SCALE * jnp.dot(weights, other_text, preferred_element_type=jnp.float32)
            backward = logit_block(other_image, own_text)
            back_weights = (jax.nn.sigmoid(backward) - diagonal).astype(jnp.bfloat16)
            text_share = (LOGIT_SCALE * lax.dot_general(back_weights, other_image, CONTRACT_ROWS, preferred_element_type=jnp.float32)).astype(jnp.bfloat16)
            text_total = text_total + lax.optimization_barrier(text_share).astype(jnp.float32)
        start_row = (device * B).astype(jnp.int32)
        image_rows = lax.dynamic_slice_in_dim(image_unit, start_row, B, 0)
        image_scale = lax.dynamic_slice_in_dim(image_inverse, start_row, B, 0)
        text_rows = lax.dynamic_slice_in_dim(text_unit, start_row, B, 0)
        text_scale = lax.dynamic_slice_in_dim(text_inverse, start_row, B, 0)
        return (row_losses / B, raw_gradient(image_rows, image_scale, image_total), raw_gradient(text_rows, text_scale, text_total))
    losses, image_grads, text_grads = lax.map(per_device, jnp.arange(devices_all, dtype=jnp.int32))
    return (losses.reshape(-1), image_grads.reshape(-1, D), text_grads.reshape(-1, D))
```

```python
import jax
import jax.numpy as jnp
from jax import lax
from jax.sharding import Mesh
from jax.sharding import PartitionSpec as P

LOGIT_SCALE = 8.0
LOGIT_BIAS = -4.0
EPSILON = 1e-06
ROW_COL = (((1,), (1,)), ((), ()))
SWAP = ((0, 1), (1, 0))
AXES = ("outer", "core", "x_hi", "z_hi", "z_lo")


def swap(value, axis):
    return lax.ppermute(value, axis, SWAP)


def normalize_rows(raw_rows):
    widened = raw_rows.astype(jnp.float32)
    inverse = lax.rsqrt(jnp.sum(widened * widened, axis=1, keepdims=True) + EPSILON)
    return (widened * inverse, inverse)


def logit_block(left_rows, right_rows):
    product = lax.dot_general(left_rows, right_rows, ROW_COL, preferred_element_type=jnp.float32)
    return LOGIT_SCALE * product + LOGIT_BIAS


def raw_gradient(normed, inverse, gradient):
    return inverse * (gradient - normed * jnp.sum(normed * gradient, axis=1, keepdims=True))


def shards(image, text):
    rows = image.shape[0]
    z_text = swap(text, "z_lo")
    x_image = swap(image, "x_hi")
    mate = swap(jnp.concatenate([image, text], axis=0), "core")
    far = swap(jnp.concatenate([x_image, z_text], axis=0), "core")

    def unit(raw):
        return normalize_rows(raw)[0].astype(jnp.bfloat16)

    mate, far = unit(mate), unit(far)
    own_image, own_text, x_image, z_text = unit(image), unit(text), unit(x_image), unit(z_text)
    mate_image, mate_text = mate[:rows], mate[rows:]
    far_image, far_text = far[:rows], far[rows:]
    r = lax.broadcasted_iota(jnp.int32, (rows, rows), 0)
    c = lax.broadcasted_iota(jnp.int32, (rows, rows), 1)
    identity = (r == c).astype(jnp.float32)

    def group(left, rights, positive, losses):
        total, loss = 0.0, 0.0
        for n, right in enumerate(rights):
            logits = logit_block(left, right)
            weights = jax.nn.sigmoid(logits)
            if losses:
                soft = jnp.log1p(jnp.exp(logits))
                if positive and n == 0:
                    soft = soft - identity * logits
                loss = loss + jnp.sum(soft, axis=1)
            if positive and n == 0:
                weights = weights - identity
            weights = weights.astype(jnp.bfloat16)
            total = total + jnp.dot(weights, right, preferred_element_type=jnp.float32)
        return LOGIT_SCALE * total, loss

    x_total, x_loss = group(x_image, [mate_text, z_text, far_text], False, True)
    x_back = swap(x_total.astype(jnp.bfloat16), "x_hi")
    z_total, _ = group(z_text, [own_image, mate_image, x_image, far_image], False, False)
    z_back = swap(z_total.astype(jnp.bfloat16), "z_lo")
    l_back = swap(x_loss, "x_hi")
    i_total, i_loss = group(own_image, [own_text, mate_text, z_text, far_text], True, True)
    t_total, _ = group(own_text, [own_image, mate_image, far_image], True, False)

    i_total = i_total + x_back.astype(jnp.float32)
    t_total = t_total + z_back.astype(jnp.float32)
    image_unit, image_inverse = normalize_rows(image)
    text_unit, text_inverse = normalize_rows(text)
    image_grad = raw_gradient(image_unit, image_inverse, i_total)
    text_grad = raw_gradient(text_unit, text_inverse, t_total)
    return ((i_loss + l_back) / rows, image_grad, text_grad)


def solution(mesh):
    n_row, n_col = mesh.devices.shape
    fine = Mesh(mesh.devices.reshape(n_row // 2, 2, 2, n_col // 4, 2), AXES)
    return jax.shard_map(
        shards,
        mesh=fine,
        in_specs=(P(AXES, None), P(AXES, None)),
        out_specs=(P(AXES), P(AXES, None), P(AXES, None)),
        check_vma=False,
    )
```

```python
import jax
import jax.numpy as jnp
from jax import lax
from jax.experimental import pallas as pl
from jax.experimental.pallas import tpu as pltpu
from jax.sharding import Mesh
from jax.sharding import PartitionSpec as P

LOGIT_SCALE = 8.0
LOGIT_BIAS = -4.0
EPSILON = 1e-06
ROW_COL = (((1,), (1,)), ((), ()))
PLAIN = (((1,), (0,)), ((), ()))
SWAP = ((0, 1), (1, 0))
AXES = ("outer", "core", "x_hi", "z_hi", "z_lo")
F32, BF16 = jnp.float32, jnp.bfloat16
MIB = 1024 * 1024


def swap(value, axis):
    return lax.ppermute(value, axis, SWAP)


def call(body, shapes, args, edges=0):
    spec = pl.BlockSpec(memory_space=pltpu.VMEM)
    rows, depth = args[0].shape[-2:]
    nbytes = sum(a.size * a.dtype.itemsize for a in args)
    return pl.pallas_call(
        body,
        out_shape=[jax.ShapeDtypeStruct(s, d) for s, d in shapes],
        in_specs=[spec] * len(args),
        out_specs=[spec] * len(shapes),
        compiler_params=pltpu.CompilerParams(vmem_limit_bytes=40 * MIB),
        cost_estimate=pl.CostEstimate(
            flops=max(1, edges) * 4 * 320 * 320 * depth, bytes_accessed=nbytes, transcendentals=0
        ),
    )(*args)


def normalize_rows(raw_rows):
    widened = raw_rows.astype(F32)
    inverse = lax.rsqrt(jnp.sum(widened * widened, axis=1, keepdims=True) + EPSILON)
    return (widened * inverse, inverse)


def norm_two(first, second, out):
    rows = first.shape[0]
    out[pl.ds(0, rows), :] = normalize_rows(first[...])[0].astype(BF16)
    out[pl.ds(rows, rows), :] = normalize_rows(second[...])[0].astype(BF16)


def eye(rows):
    r = lax.broadcasted_iota(jnp.int32, (rows, rows), 0)
    c = lax.broadcasted_iota(jnp.int32, (rows, rows), 1)
    return r == c


def as_row(column):
    return jnp.sum(jnp.where(eye(column.shape[0]), column, 0.0), axis=0, keepdims=True)


def edge(left, right, positive=False, losses=False):
    logits = lax.dot_general(left, right, ROW_COL, preferred_element_type=F32)
    logits = LOGIT_SCALE * logits + LOGIT_BIAS
    grown = jnp.exp(logits)
    whole = 1.0 + grown
    part = 1.0 / whole
    weights = grown * part
    loss = None
    if losses:
        soft = jnp.log(whole) + (grown - (whole - 1.0)) * part
        if positive:
            soft = jnp.where(eye(left.shape[0]), soft - logits, soft)
        loss = jnp.sum(soft, axis=1, keepdims=True)
    if positive:
        weights = jnp.where(eye(left.shape[0]), weights - 1.0, weights)
    share = lax.dot_general(weights.astype(BF16), right, PLAIN, preferred_element_type=F32)
    return share, loss


def own_body(own, mate, i_out, t_out, loss_out):
    rows = i_out.shape[0]
    image, text = own[pl.ds(0, rows), :], own[pl.ds(rows, rows), :]
    mate_image, mate_text = mate[pl.ds(0, rows), :], mate[pl.ds(rows, rows), :]
    first, loss = edge(image, text, True, True)
    second, more = edge(image, mate_text, False, True)
    i_out[...] = first + second
    loss_out[...] = as_row(loss + more)
    first, _ = edge(text, image, True)
    second, _ = edge(text, mate_image)
    t_out[...] = first + second


def mid_body(own, mate, near, x_out, z_out, loss_out):
    rows = x_out.shape[0]
    image, mate_image, mate_text = own[pl.ds(0, rows), :], mate[pl.ds(0, rows), :], mate[pl.ds(rows, rows), :]
    x_image, z_text = near[pl.ds(0, rows), :], near[pl.ds(rows, rows), :]
    first, loss = edge(x_image, mate_text, False, True)
    second, more = edge(x_image, z_text, False, True)
    x_out[...] = first + second
    loss_out[...] = as_row(loss + more)
    total = edge(z_text, image)[0] + edge(z_text, mate_image)[0] + edge(z_text, x_image)[0]
    z_out[...] = total


def back_body(near, far, x_in, z_in, loss_in, x_out, z_out, loss_out):
    rows = x_out.shape[0]
    x_image, z_text = near[pl.ds(0, rows), :], near[pl.ds(rows, rows), :]
    far_image, far_text = far[pl.ds(0, rows), :], far[pl.ds(rows, rows), :]
    share, loss = edge(x_image, far_text, False, True)
    x_out[...] = (LOGIT_SCALE * (x_in[...] + share)).astype(BF16)
    loss_out[...] = loss_in[...] + as_row(loss)
    share, _ = edge(z_text, far_image)
    z_out[...] = (LOGIT_SCALE * (z_in[...] + share)).astype(BF16)


def rest_body(own, near, far, i_in, t_in, loss_in, i_out, t_out, loss_out):
    rows = i_out.shape[0]
    image, text = own[pl.ds(0, rows), :], own[pl.ds(rows, rows), :]
    z_text = near[pl.ds(rows, rows), :]
    far_image, far_text = far[pl.ds(0, rows), :], far[pl.ds(rows, rows), :]
    first, loss = edge(image, z_text, False, True)
    second, more = edge(image, far_text, False, True)
    i_out[...] = i_in[...] + first + second
    loss_out[...] = loss_in[...] + as_row(loss + more)
    t_out[...] = t_in[...] + edge(text, far_image)[0]


def raw_gradient(raw, total, back):
    unit, inverse = normalize_rows(raw)
    gradient = LOGIT_SCALE * total + back.astype(F32)
    return inverse * (gradient - unit * jnp.sum(unit * gradient, axis=1, keepdims=True))


def last_body(image, text, i_in, t_in, x_back, z_back, loss_in, loss_back, loss_out, i_out, t_out):
    loss_out[...] = (loss_in[...] + loss_back[...]) * (1.0 / image.shape[0])
    i_out[...] = raw_gradient(image[...], i_in[...], x_back[...])
    t_out[...] = raw_gradient(text[...], t_in[...], z_back[...])


def shards(image, text):
    rows, depth = image.shape
    pair, block, line = (2 * rows, depth), (rows, depth), (1, rows)
    x_image = swap(image, "x_hi")
    z_text = swap(text, "z_lo")
    (own,) = call(norm_two, [(pair, BF16)], (image, text))
    mate = swap(own, "core")
    i_total, t_total, i_loss = call(own_body, [(block, F32), (block, F32), (line, F32)], (own, mate), 4)
    (near,) = call(norm_two, [(pair, BF16)], (x_image, z_text))
    far = swap(near, "core")
    x_total, z_total, x_loss = call(
        mid_body, [(block, F32), (block, F32), (line, F32)], (own, mate, near), 5
    )
    x_share, z_share, x_loss = call(
        back_body, [(block, BF16), (block, BF16), (line, F32)], (near, far, x_total, z_total, x_loss), 2
    )
    x_back = swap(x_share, "x_hi")
    z_back = swap(z_share, "z_lo")
    loss_back = swap(x_loss, "x_hi")
    i_total, t_total, i_loss = call(
        rest_body, [(block, F32), (block, F32), (line, F32)], (own, near, far, i_total, t_total, i_loss), 3
    )
    loss, image_grad, text_grad = call(
        last_body,
        [(line, F32), (block, F32), (block, F32)],
        (image, text, i_total, t_total, x_back, z_back, i_loss, loss_back),
    )
    return (loss.reshape(rows), image_grad, text_grad)


def solution(mesh):
    n_row, n_col = mesh.devices.shape
    fine = Mesh(mesh.devices.reshape(n_row // 2, 2, 2, n_col // 4, 2), AXES)
    return jax.shard_map(
        shards,
        mesh=fine,
        in_specs=(P(AXES, None), P(AXES, None)),
        out_specs=(P(AXES), P(AXES, None), P(AXES, None)),
        check_vma=False,
    )
```

```python
import math
from functools import partial

import jax
import jax.numpy as jnp
from jax import lax
from jax.experimental import pallas as pl
from jax.experimental.pallas import tpu as pltpu
from jax.sharding import Mesh
from jax.sharding import PartitionSpec as P

LOGIT_SCALE = 8.0
LOGIT_BIAS = -4.0
EPSILON = 1e-06
LOG2E = math.log2(math.e)
LANES = 128
ROW_COL = (((1,), (1,)), ((), ()))
PLAIN = (((1,), (0,)), ((), ()))
SWAP = ((0, 1), (1, 0))
AXES = ("outer", "core", "x_hi", "z_hi", "z_lo")
F32, BF16 = jnp.float32, jnp.bfloat16
MIB = 1024 * 1024
TOKEN = ((8, LANES), F32)


def swap(value, axis):
    return lax.ppermute(value, axis, SWAP)


def call(body, shapes, args, far_outs=(), scratch=()):
    vmem, far = pl.BlockSpec(memory_space=pltpu.VMEM), pl.BlockSpec(memory_space=pl.ANY)
    return pl.pallas_call(
        body,
        out_shape=[jax.ShapeDtypeStruct(s, d) for s, d in shapes],
        in_specs=[vmem] * len(args),
        out_specs=[far if n in far_outs else vmem for n in range(len(shapes))],
        scratch_shapes=scratch,
        compiler_params=pltpu.CompilerParams(vmem_limit_bytes=32 * MIB),
        cost_estimate=pl.CostEstimate(flops=1, bytes_accessed=1, transcendentals=0),
    )(*args)


def normalize_rows(raw_rows):
    widened = raw_rows.astype(F32)
    inverse = lax.rsqrt(jnp.sum(widened * widened, axis=1, keepdims=True) + EPSILON)
    return (widened * inverse, inverse)


def norm_body(*refs):
    pieces, out = refs[:-1], refs[-1]
    rows = pieces[0].shape[0]
    for n, piece in enumerate(pieces):
        out[pl.ds(n * rows, rows), :] = normalize_rows(piece[...])[0].astype(BF16)


def as_row(column):
    rows = column.shape[0]
    r = lax.broadcasted_iota(jnp.int32, (rows, rows), 0)
    c = lax.broadcasted_iota(jnp.int32, (rows, rows), 1)
    return jnp.sum(jnp.where(r == c, column, 0.0), axis=0, keepdims=True)


def soft_sum(grown, whole):
    total, groups = 0.0, grown.shape[1] // LANES
    carried = grown[:, :LANES]
    for n in range(1, groups):
        part = slice(n * LANES, (n + 1) * LANES)
        carried = carried * whole[:, part] + grown[:, part]
    total = jnp.sum(jnp.log1p(carried), axis=1, keepdims=True)
    if groups * LANES < grown.shape[1]:
        total = total + jnp.sum(jnp.log1p(grown[:, groups * LANES :]), axis=1, keepdims=True)
    return total


def edges(left, rights, positive=False, losses=False):
    right = jnp.concatenate(rights, axis=0)
    product = lax.dot_general(left, right, ROW_COL, preferred_element_type=F32)
    grown = jnp.exp2(product * (LOGIT_SCALE * LOG2E) + LOGIT_BIAS * LOG2E)
    whole = 1.0 + grown
    weights = grown * pltpu.reciprocal(whole, approx=True)
    if positive:
        r = lax.broadcasted_iota(jnp.int32, product.shape, 0)
        c = lax.broadcasted_iota(jnp.int32, product.shape, 1)
        weights = jnp.where(r == c, weights - 1.0, weights)
    share = lax.dot_general(weights.astype(BF16), right, PLAIN, preferred_element_type=F32)
    if not losses:
        return share
    loss = soft_sum(grown, whole)
    if positive:
        logits = LOGIT_SCALE * product + LOGIT_BIAS
        loss = loss - jnp.sum(jnp.where(r == c, logits, 0.0), axis=1, keepdims=True)
    return share, loss


def halves(ref):
    rows = ref.shape[0] // 2
    return ref[pl.ds(0, rows), :], ref[pl.ds(rows, rows), :]


def z_body(own, mate, x_near, x_far, z_near, share, token):
    image, mate_image = halves(own)[0], halves(mate)[0]
    total = edges(z_near[...], [image, mate_image, x_near[...], x_far[...]])
    share[...] = (LOGIT_SCALE * total).astype(BF16)
    token[...] = jnp.zeros(token.shape, F32)


def x_body(mate, x_near, z_near, z_far, _, share, loss):
    total, loss[...] = edges(x_near[...], [halves(mate)[1], z_near[...], z_far[...]], False, True)
    share[...] = (LOGIT_SCALE * total).astype(BF16)


def own_body(own, mate, x_far, z_near, z_far, x_loss, i_out, t_out, loss_out, x_loss_out):
    x_loss_out[...] = as_row(x_loss[...])
    image, text = halves(own)
    mate_image, mate_text = halves(mate)
    total, loss = edges(image, [text, mate_text, z_near[...], z_far[...]], True, True)
    i_out[...] = LOGIT_SCALE * total
    loss_out[...] = as_row(loss)
    t_out[...] = LOGIT_SCALE * edges(text, [image, mate_image, x_far[...]], True)


def raw_gradient(raw, gradient):
    unit, inverse = normalize_rows(raw)
    return inverse * (gradient - unit * jnp.sum(unit * gradient, axis=1, keepdims=True))


def last_body(raw, total, back, *rest):
    out, held, sems = rest[-3:]
    pieces = sems.shape[0]
    rows = raw.shape[0] // pieces
    copies = []
    for n in range(pieces):
        part = pl.ds(n * rows, rows)
        held[part, :] = raw_gradient(raw[part, :], total[part, :] + back[part, :].astype(F32))
        copies.append(pltpu.make_async_copy(held.at[part, :], out.at[part, :], sems.at[n]))
        copies[-1].start()
    for copy in copies:
        copy.wait()


def last(raw, total, back, *tokens):
    return call(
        last_body,
        [(raw.shape, F32)],
        (raw, total, back) + tokens,
        far_outs=(0,),
        scratch=[pltpu.VMEM(raw.shape, F32), pltpu.SemaphoreType.DMA((4,))],
    )[0]


def shards(image, text):
    rows, depth = image.shape
    block, pair = (rows, depth), (2 * rows, depth)
    x_near, z_near = swap(image, "x_hi"), swap(text, "z_lo")
    (own,) = call(norm_body, [(pair, BF16)], (image, text))
    mate = swap(own, "core")
    (x_near,) = call(norm_body, [(block, BF16)], (x_near,))
    x_far = swap(x_near, "core")
    (z_near,) = call(norm_body, [(block, BF16)], (z_near,))
    z_far = swap(z_near, "core")
    z_share, token = call(z_body, [(block, BF16), TOKEN], (own, mate, x_near, x_far, z_near))
    z_back = swap(z_share, "z_lo")
    x_share, x_loss = call(
        x_body, [(block, BF16), ((rows, 1), F32)], (mate, x_near, z_near, z_far, token)
    )
    x_back = swap(x_share, "x_hi")
    i_total, t_total, i_loss, x_loss = call(
        own_body,
        [(block, F32), (block, F32), ((1, rows), F32), ((1, rows), F32)],
        (own, mate, x_far, z_near, z_far, x_loss),
    )
    loss = ((i_loss + swap(x_loss, "x_hi")) * (1.0 / rows)).reshape(rows)
    text_grad = last(text, t_total, z_back)
    image_grad = last(image, i_total, x_back)
    return (loss, image_grad, text_grad)


def solution(mesh):
    n_row, n_col = mesh.devices.shape
    fine = Mesh(mesh.devices.reshape(n_row // 2, 2, 2, n_col // 4, 2), AXES)
    return jax.shard_map(
        shards,
        mesh=fine,
        in_specs=(P(AXES, None), P(AXES, None)),
        out_specs=(P(AXES), P(AXES, None), P(AXES, None)),
        check_vma=False,
    )
```

```python
import math
from functools import partial

import jax
import jax.numpy as jnp
from jax import lax
from jax.experimental import pallas as pl
from jax.experimental.pallas import tpu as pltpu
from jax.sharding import Mesh
from jax.sharding import PartitionSpec as P

LOGIT_SCALE = 8.0
LOGIT_BIAS = -4.0
EPSILON = 1e-06
LOG2E = math.log2(math.e)
LANES = 128
ROW_COL = (((1,), (1,)), ((), ()))
PLAIN = (((1,), (0,)), ((), ()))
SWAP = ((0, 1), (1, 0))
AXES = ("outer", "core", "x_hi", "z_hi", "z_lo")
F32, BF16 = jnp.float32, jnp.bfloat16
MIB = 1024 * 1024
TOKEN = ((8, LANES), F32)
FIRST = 192


def swap(value, axis):
    return lax.ppermute(value, axis, SWAP)


def call(body, shapes, args, far_args=(), far_outs=(), scratch=(), aliases=None, flops=1):
    vmem, far = pl.BlockSpec(memory_space=pltpu.VMEM), pl.BlockSpec(memory_space=pl.ANY)
    return pl.pallas_call(
        body,
        out_shape=[jax.ShapeDtypeStruct(s, d) for s, d in shapes],
        in_specs=[far if n in far_args else vmem for n in range(len(args))],
        out_specs=[far if n in far_outs else vmem for n in range(len(shapes))],
        scratch_shapes=scratch,
        input_output_aliases=aliases or {},
        compiler_params=pltpu.CompilerParams(vmem_limit_bytes=32 * MIB),
        cost_estimate=pl.CostEstimate(flops=flops, bytes_accessed=1, transcendentals=0),
    )(*args)


def normalize_rows(raw_rows):
    widened = raw_rows.astype(F32)
    inverse = lax.rsqrt(jnp.sum(widened * widened, axis=1, keepdims=True) + EPSILON)
    return (widened * inverse, inverse)


def norm_body(*refs):
    pieces, out = refs[:-1], refs[-1]
    rows = pieces[0].shape[0]
    for n, piece in enumerate(pieces):
        out[pl.ds(n * rows, rows), :] = normalize_rows(piece[...])[0].astype(BF16)


def own_norm(image, text, out, image_held, text_held):
    norm_body(image, text, out)
    image_held[...] = image[...]
    text_held[...] = text[...]


def as_row(column):
    rows = column.shape[0]
    r = lax.broadcasted_iota(jnp.int32, (rows, rows), 0)
    c = lax.broadcasted_iota(jnp.int32, (rows, rows), 1)
    return jnp.sum(jnp.where(r == c, column, 0.0), axis=0, keepdims=True)


def soft_sum(grown, whole):
    total, groups = 0.0, grown.shape[1] // LANES
    carried = grown[:, :LANES]
    for n in range(1, groups):
        part = slice(n * LANES, (n + 1) * LANES)
        carried = carried * whole[:, part] + grown[:, part]
    total = jnp.sum(jnp.log1p(carried), axis=1, keepdims=True)
    if groups * LANES < grown.shape[1]:
        total = total + jnp.sum(jnp.log1p(grown[:, groups * LANES :]), axis=1, keepdims=True)
    return total


def edges(left, rights, positive=False, losses=False):
    right = jnp.concatenate(rights, axis=0)
    product = lax.dot_general(left, right, ROW_COL, preferred_element_type=F32)
    grown = jnp.exp2(product * (LOGIT_SCALE * LOG2E) + LOGIT_BIAS * LOG2E)
    whole = 1.0 + grown
    weights = grown * pltpu.reciprocal(whole, approx=True)
    if positive:
        r = lax.broadcasted_iota(jnp.int32, product.shape, 0)
        c = lax.broadcasted_iota(jnp.int32, product.shape, 1)
        weights = jnp.where(r == c, weights - 1.0, weights)
    share = lax.dot_general(weights.astype(BF16), right, PLAIN, preferred_element_type=F32)
    if not losses:
        return share
    loss = soft_sum(grown, whole)
    if positive:
        logits = LOGIT_SCALE * product + LOGIT_BIAS
        loss = loss - jnp.sum(jnp.where(r == c, logits, 0.0), axis=1, keepdims=True)
    return share, loss


def halves(ref):
    rows = ref.shape[0] // 2
    return ref[pl.ds(0, rows), :], ref[pl.ds(rows, rows), :]


def z_body(own, mate, x_near, x_far, z_near, share, token):
    image, mate_image = halves(own)[0], halves(mate)[0]
    total = edges(z_near[...], [image, mate_image, x_near[...], x_far[...]])
    share[...] = (LOGIT_SCALE * total).astype(BF16)
    token[...] = jnp.zeros(token.shape, F32)


def x_body(start, mate, x_near, z_near, z_far, _, share, loss, token):
    left = x_near[pl.ds(start, share.shape[0]), :]
    total, loss[...] = edges(left, [halves(mate)[1], z_near[...], z_far[...]], False, True)
    share[...] = (LOGIT_SCALE * total).astype(BF16)
    token[...] = jnp.zeros(token.shape, F32)


def own_body(own, mate, x_far, z_near, z_far, x_loss_1, x_loss_2, i_out, t_out, loss_out, x_loss):
    x_loss[...] = as_row(jnp.concatenate([x_loss_1[...], x_loss_2[...]], axis=0))
    image, text = halves(own)
    mate_image, mate_text = halves(mate)
    total, loss = edges(image, [text, mate_text, z_near[...], z_far[...]], True, True)
    i_out[...] = LOGIT_SCALE * total
    loss_out[...] = as_row(loss)
    t_out[...] = LOGIT_SCALE * edges(text, [image, mate_image, x_far[...]], True)


def raw_gradient(raw, gradient):
    unit, inverse = normalize_rows(raw)
    return inverse * (gradient - unit * jnp.sum(unit * gradient, axis=1, keepdims=True))


def finish(start, raw, total, back, out, held, sems):
    pieces = sems.shape[0]
    rows = held.shape[0] // pieces
    copies = []
    for n in range(pieces):
        part, at = pl.ds(n * rows, rows), pl.ds(start + n * rows, rows)
        held[part, :] = raw_gradient(raw[at, :], total[at, :] + back[part, :].astype(F32))
        copies.append(pltpu.make_async_copy(held.at[part, :], out.at[at, :], sems.at[n]))
        copies[-1].start()
    return copies


def last_body(raw, total, back, _, out, token, held, sems):
    token[...] = jnp.zeros(token.shape, F32)
    for copy in finish(0, raw, total, back, out, held, sems):
        copy.wait()


def end_body(raw, total, back, i_loss, loss_back, *rest):
    out, loss_out, held, sems, held_loss, loss_sem = rest[-6:]
    rows = raw.shape[0]
    held_loss[...] = ((i_loss[...] + loss_back[...]) * (1.0 / rows)).reshape(held_loss.shape)
    copies = [pltpu.make_async_copy(held_loss, loss_out, loss_sem)]
    copies[0].start()
    for copy in copies + finish(rows - back.shape[0], raw, total, back, out, held, sems):
        copy.wait()


def last(raw, total, back, token, before=None, losses=()):
    pieces = back.shape[0] // 32
    shapes = [(raw.shape, F32), TOKEN]
    scratch = [pltpu.VMEM(back.shape, F32), pltpu.SemaphoreType.DMA((pieces,))]
    if before is None:
        return call(last_body, shapes, (raw, total, back, token), far_outs=(0,), scratch=scratch)
    line = (raw.shape[0],)
    return call(
        end_body,
        [shapes[0], (line, F32)],
        (raw, total, back, *losses, token, before),
        far_args=(6,),
        far_outs=(0, 1),
        scratch=scratch + [pltpu.VMEM(line, F32), pltpu.SemaphoreType.DMA],
        aliases={6: 0},
    )


def shards(image, text):
    rows, depth = image.shape
    block, pair = (rows, depth), (2 * rows, depth)
    x_near, z_near = swap(image, "x_hi"), swap(text, "z_lo")
    own, image, text = call(own_norm, [(pair, BF16), (block, BF16), (block, BF16)], (image, text))
    mate = swap(own, "core")
    (x_near,) = call(norm_body, [(block, BF16)], (x_near,))
    x_far = swap(x_near, "core")
    (z_near,) = call(norm_body, [(block, BF16)], (z_near,), flops=4*10**9)
    z_far = swap(z_near, "core")
    z_share, token = call(z_body, [(block, BF16), TOKEN], (own, mate, x_near, x_far, z_near))
    z_back = swap(z_share, "z_lo")
    backs, losses = [], []
    for start, count in ((0, FIRST), (FIRST, rows - FIRST)):
        x_share, loss, token = call(
            partial(x_body, start),
            [((count, depth), BF16), ((count, 1), F32), TOKEN],
            (mate, x_near, z_near, z_far, token),
        )
        backs.append(swap(x_share, "x_hi"))
        losses.append(loss)
    i_total, t_total, i_loss, x_loss = call(
        own_body,
        [(block, F32), (block, F32), ((1, rows), F32), ((1, rows), F32)],
        (own, mate, x_far, z_near, z_far, *losses),
    )
    loss_back = swap(x_loss, "x_hi")
    image_grad, token = last(image, i_total, backs[0], token)
    text_grad, token = last(text, t_total, z_back, token)
    image_grad, loss = last(image, i_total, backs[1], token, image_grad, (i_loss, loss_back))
    return (loss, image_grad, text_grad)


def solution(mesh):
    n_row, n_col = mesh.devices.shape
    fine = Mesh(mesh.devices.reshape(n_row // 2, 2, 2, n_col // 4, 2), AXES)
    return jax.shard_map(
        shards,
        mesh=fine,
        in_specs=(P(AXES, None), P(AXES, None)),
        out_specs=(P(AXES), P(AXES, None), P(AXES, None)),
        check_vma=False,
    )
```

```python
import math
from functools import partial

import jax
import jax.numpy as jnp
from jax import lax
from jax.experimental import pallas as pl
from jax.experimental.pallas import tpu as pltpu
from jax.sharding import Mesh
from jax.sharding import PartitionSpec as P

LOGIT_SCALE = 8.0
LOGIT_BIAS = -4.0
EPSILON = 1e-06
LOG2E = math.log2(math.e)
LANES = 128
ROW_COL = (((1,), (1,)), ((), ()))
PLAIN = (((1,), (0,)), ((), ()))
SWAP = ((0, 1), (1, 0))
AXES = ("outer", "core", "x_hi", "z_hi", "z_lo")
F32, BF16 = jnp.float32, jnp.bfloat16
MIB = 1024 * 1024
TOKEN = ((8, LANES), F32)
FIRST = 192
PACK = 16


def swap(value, axis):
    return lax.ppermute(value, axis, SWAP)


def call(body, shapes, args, far_args=(), far_outs=(), scratch=(), aliases=None, flops=1):
    vmem, far = pl.BlockSpec(memory_space=pltpu.VMEM), pl.BlockSpec(memory_space=pl.ANY)
    return pl.pallas_call(
        body,
        out_shape=[jax.ShapeDtypeStruct(s, d) for s, d in shapes],
        in_specs=[far if n in far_args else vmem for n in range(len(args))],
        out_specs=[far if n in far_outs else vmem for n in range(len(shapes))],
        scratch_shapes=scratch,
        input_output_aliases=aliases or {},
        compiler_params=pltpu.CompilerParams(vmem_limit_bytes=32 * MIB),
        cost_estimate=pl.CostEstimate(flops=flops, bytes_accessed=1, transcendentals=0),
    )(*args)


def normalize_rows(raw_rows):
    widened = raw_rows.astype(F32)
    inverse = lax.rsqrt(jnp.sum(widened * widened, axis=1, keepdims=True) + EPSILON)
    return (widened * inverse, inverse)


def norm_body(*refs):
    pieces, out = refs[:-1], refs[-1]
    rows = pieces[0].shape[0]
    for n, piece in enumerate(pieces):
        out[pl.ds(n * rows, rows), :] = normalize_rows(piece[...])[0].astype(BF16)


def norm_after(raw, _, out):
    norm_body(raw, out)


def own_norm(image, text, out, image_held, text_held):
    norm_body(image, text, out)
    image_held[...] = image[...]
    text_held[...] = text[...]


def as_row(column):
    rows = column.shape[0]
    r = lax.broadcasted_iota(jnp.int32, (rows, rows), 0)
    c = lax.broadcasted_iota(jnp.int32, (rows, rows), 1)
    return jnp.sum(jnp.where(r == c, column, 0.0), axis=0, keepdims=True)


def soft_sum(grown, whole):
    total, groups = 0.0, grown.shape[1] // LANES
    carried = grown[:, :LANES]
    for n in range(1, groups):
        part = slice(n * LANES, (n + 1) * LANES)
        carried = carried * whole[:, part] + grown[:, part]
    total = jnp.sum(jnp.log1p(carried), axis=1, keepdims=True)
    if groups * LANES < grown.shape[1]:
        total = total + jnp.sum(jnp.log1p(grown[:, groups * LANES :]), axis=1, keepdims=True)
    return total


def edges(left, rights, positive=False, losses=False):
    right = jnp.concatenate(rights, axis=0)
    product = lax.dot_general(left, right, ROW_COL, preferred_element_type=F32)
    grown = jnp.exp2(product * (LOGIT_SCALE * LOG2E) + LOGIT_BIAS * LOG2E)
    whole = 1.0 + grown
    weights = grown * pltpu.reciprocal(whole, approx=True)
    if positive:
        r = lax.broadcasted_iota(jnp.int32, product.shape, 0)
        c = lax.broadcasted_iota(jnp.int32, product.shape, 1)
        weights = jnp.where(r == c, weights - 1.0, weights)
    share = lax.dot_general(weights.astype(BF16), right, PLAIN, preferred_element_type=F32)
    if not losses:
        return share
    loss = soft_sum(grown, whole)
    if positive:
        logits = LOGIT_SCALE * product + LOGIT_BIAS
        loss = loss - jnp.sum(jnp.where(r == c, logits, 0.0), axis=1, keepdims=True)
    return share, loss


def halves(ref):
    rows = ref.shape[0] // 2
    return ref[pl.ds(0, rows), :], ref[pl.ds(rows, rows), :]


def in_parts(row):
    high = row.astype(BF16).astype(F32)
    middle = (row - high).astype(BF16).astype(F32)
    r = lax.broadcasted_iota(jnp.int32, (PACK, row.shape[1]), 0)
    low = jnp.where(r == 2, row - high - middle, 0.0)
    return jnp.where(r == 0, high, jnp.where(r == 1, middle, low)).astype(BF16)


def x_first(mate, x_near, z_near, z_far, share, loss, token):
    left = x_near[pl.ds(0, share.shape[0]), :]
    total, loss[...] = edges(left, [halves(mate)[1], z_near[...], z_far[...]], False, True)
    share[...] = (LOGIT_SCALE * total).astype(BF16)
    token[...] = jnp.zeros(token.shape, F32)


def x_second(mate, x_near, z_near, z_far, lost, _, share, token):
    rows = share.shape[0] - PACK
    left = x_near[pl.ds(x_near.shape[0] - rows, rows), :]
    total, loss = edges(left, [halves(mate)[1], z_near[...], z_far[...]], False, True)
    share[pl.ds(0, rows), :] = (LOGIT_SCALE * total).astype(BF16)
    share[pl.ds(rows, PACK), :] = jnp.zeros((PACK, share.shape[1]), BF16)
    row = as_row(jnp.concatenate([lost[...], loss], axis=0))
    share[pl.ds(rows, PACK), pl.ds(0, row.shape[1])] = in_parts(row)
    token[...] = jnp.zeros(token.shape, F32)


def mid_body(own, z_near, out, token):
    out[...] = edges(z_near[...], [halves(own)[0]])
    token[...] = jnp.zeros(token.shape, F32)


def z_body(start, mate, x_near, x_far, z_near, begun, _, share, token):
    part = pl.ds(start, share.shape[0])
    total = edges(z_near[part, :], [halves(mate)[0], x_near[...], x_far[...]])
    share[...] = (LOGIT_SCALE * (begun[part, :] + total)).astype(BF16)
    token[...] = jnp.zeros(token.shape, F32)


def own_body(own, mate, x_far, z_near, z_far, _, i_out, t_out, loss_out):
    image, text = halves(own)
    mate_image, mate_text = halves(mate)
    total, loss = edges(image, [text, mate_text, z_near[...], z_far[...]], True, True)
    i_out[...] = LOGIT_SCALE * total
    loss_out[...] = as_row(loss)
    t_out[...] = LOGIT_SCALE * edges(text, [image, mate_image, x_far[...]], True)


def raw_gradient(raw, gradient):
    unit, inverse = normalize_rows(raw)
    return inverse * (gradient - unit * jnp.sum(unit * gradient, axis=1, keepdims=True))


def finish(start, raw, total, back, out, held, sems):
    pieces = sems.shape[0]
    rows = held.shape[0] // pieces
    copies = []
    for n in range(pieces):
        part, at = pl.ds(n * rows, rows), pl.ds(start + n * rows, rows)
        held[part, :] = raw_gradient(raw[at, :], total[at, :] + back[part, :].astype(F32))
        copies.append(pltpu.make_async_copy(held.at[part, :], out.at[at, :], sems.at[n]))
        copies[-1].start()
    return copies


def last_body(start, raw, total, back, *rest):
    token, out, held, sems = rest[-4:]
    token[...] = jnp.zeros(token.shape, F32)
    for copy in finish(start, raw, total, back, out, held, sems):
        copy.wait()


def final_body(start, raw, total, back, *rest):
    out, held, sems = rest[-3:]
    for copy in finish(start, raw, total, back, out, held, sems):
        copy.wait()


def loss_body(start, raw, total, back, i_loss, *rest):
    loss_out, token, out, held, sems, held_loss, loss_sem = rest[-7:]
    token[...] = jnp.zeros(token.shape, F32)
    rows = raw.shape[0]
    parts = back[pl.ds(rows - start, PACK), :].astype(F32)[:, :rows]
    loss = (i_loss[...] + jnp.sum(parts, axis=0, keepdims=True)) * (1.0 / rows)
    held_loss[...] = loss.reshape(held_loss.shape)
    copies = [pltpu.make_async_copy(held_loss, loss_out, loss_sem)]
    copies[0].start()
    for copy in copies + finish(start, raw, total, back, out, held, sems):
        copy.wait()


def last(start, count, raw, total, back, token, before=(), i_loss=()):
    args = (raw, total, back, *i_loss, token, *before)
    shapes, far_outs = [TOKEN, (raw.shape, F32)], (1,)
    scratch = [pltpu.VMEM((count, raw.shape[1]), F32), pltpu.SemaphoreType.DMA((count // 32,))]
    if i_loss:
        line = (raw.shape[0],)
        shapes, far_outs = [(line, F32)] + shapes, (0, 2)
        scratch += [pltpu.VMEM(line, F32), pltpu.SemaphoreType.DMA]
    body = loss_body if i_loss else last_body
    if before and not i_loss:
        body, shapes, far_outs = final_body, shapes[1:], (0,)
    return call(
        partial(body, start),
        shapes,
        args,
        far_args=(len(args) - 1,) if before else (),
        far_outs=far_outs,
        scratch=scratch,
        aliases={len(args) - 1: len(shapes) - 1} if before else None,
    )


def shards(image, text):
    rows, depth = image.shape
    block, pair = (rows, depth), (2 * rows, depth)
    first, second = FIRST, rows - FIRST
    z_near, x_near = swap(text, "z_lo"), swap(image, "x_hi")
    own, image, text = call(own_norm, [(pair, BF16), (block, BF16), (block, BF16)], (image, text))
    mate = swap(own, "core")
    (z_near,) = call(norm_body, [(block, BF16)], (z_near,))
    z_far = swap(z_near, "core")
    begun, token = call(mid_body, [(block, F32), TOKEN], (own, z_near))
    (x_near,) = call(norm_after, [(block, BF16)], (x_near, token), flops=4 * 10**9)
    x_far = swap(x_near, "core")
    share, x_loss, token = call(
        x_first, [((first, depth), BF16), ((first, 1), F32), TOKEN], (mate, x_near, z_near, z_far)
    )
    x_1 = swap(share, "x_hi")
    share, token = call(
        partial(z_body, 0),
        [((first, depth), BF16), TOKEN],
        (mate, x_near, x_far, z_near, begun, token),
    )
    z_1 = swap(share, "z_lo")
    share, token = call(
        x_second,
        [((second + PACK, depth), BF16), TOKEN],
        (mate, x_near, z_near, z_far, x_loss, token),
    )
    x_2 = swap(share, "x_hi")
    share, token = call(
        partial(z_body, first),
        [((second, depth), BF16), TOKEN],
        (mate, x_near, x_far, z_near, begun, token),
    )
    z_2 = swap(share, "z_lo")
    i_total, t_total, i_loss = call(
        own_body,
        [(block, F32), (block, F32), ((1, rows), F32)],
        (own, mate, x_far, z_near, z_far, token),
    )
    token, image_grad = last(0, first, image, i_total, x_1, token)
    token, text_grad = last(0, first, text, t_total, z_1, token)
    loss, token, image_grad = last(
        first, second, image, i_total, x_2, token, (image_grad,), (i_loss,)
    )
    (text_grad,) = last(first, second, text, t_total, z_2, token, (text_grad,))
    return (loss, image_grad, text_grad)


def solution(mesh):
    n_row, n_col = mesh.devices.shape
    fine = Mesh(mesh.devices.reshape(n_row // 2, 2, 2, n_col // 4, 2), AXES)
    return jax.shard_map(
        shards,
        mesh=fine,
        in_specs=(P(AXES, None), P(AXES, None)),
        out_specs=(P(AXES), P(AXES, None), P(AXES, None)),
        check_vma=False,
    )
```

```python
import math
from functools import partial

import jax
import jax.numpy as jnp
from jax import lax
from jax.experimental import pallas as pl
from jax.experimental.pallas import tpu as pltpu
from jax.sharding import Mesh
from jax.sharding import PartitionSpec as P

LOGIT_SCALE = 8.0
LOGIT_BIAS = -4.0
EPSILON = 1e-06
LOG2E = math.log2(math.e)
LANES = 128
ROW_COL = (((1,), (1,)), ((), ()))
PLAIN = (((1,), (0,)), ((), ()))
SWAP = ((0, 1), (1, 0))
AXES = ("outer", "core", "x_hi", "z_hi", "z_lo")
F32, BF16 = jnp.float32, jnp.bfloat16
MIB = 1024 * 1024
TOKEN = ((8, LANES), F32)
FIRST = 192
PACK = 16
PIECES = 2


def swap(value, axis):
    return lax.ppermute(value, axis, SWAP)


def call(body, shapes, args, far_args=(), far_outs=(), scratch=(), aliases=None, flops=1):
    vmem, far = pl.BlockSpec(memory_space=pltpu.VMEM), pl.BlockSpec(memory_space=pl.ANY)
    return pl.pallas_call(
        body,
        out_shape=[jax.ShapeDtypeStruct(s, d) for s, d in shapes],
        in_specs=[far if n in far_args else vmem for n in range(len(args))],
        out_specs=[far if n in far_outs else vmem for n in range(len(shapes))],
        scratch_shapes=scratch,
        input_output_aliases=aliases or {},
        compiler_params=pltpu.CompilerParams(vmem_limit_bytes=32 * MIB),
        cost_estimate=pl.CostEstimate(flops=flops, bytes_accessed=1, transcendentals=0),
    )(*args)


def normalize_rows(raw_rows):
    widened = raw_rows.astype(F32)
    inverse = lax.rsqrt(jnp.sum(widened * widened, axis=1, keepdims=True) + EPSILON)
    return (widened * inverse, inverse)


def norm_body(*refs):
    pieces, out = refs[:-1], refs[-1]
    rows = pieces[0].shape[0]
    for n, piece in enumerate(pieces):
        out[pl.ds(n * rows, rows), :] = normalize_rows(piece[...])[0].astype(BF16)


def norm_after(raw, _, out):
    norm_body(raw, out)


def own_norm(image, text, out, image_held, text_held, text_unit, *pieces):
    norm_body(image, text, out)
    text_unit[...] = halves(out)[1]
    rows = pieces[0].shape[0]
    for n, piece in enumerate(pieces):
        piece[...] = out[pl.ds(n * rows, rows), :]
    image_held[...] = image[...]
    text_held[...] = text[...]


def as_row(column):
    rows = column.shape[0]
    r = lax.broadcasted_iota(jnp.int32, (rows, rows), 0)
    c = lax.broadcasted_iota(jnp.int32, (rows, rows), 1)
    return jnp.sum(jnp.where(r == c, column, 0.0), axis=0, keepdims=True)


def soft_sum(grown, whole):
    total, groups = 0.0, grown.shape[1] // LANES
    carried = grown[:, :LANES]
    for n in range(1, groups):
        part = slice(n * LANES, (n + 1) * LANES)
        carried = carried * whole[:, part] + grown[:, part]
    total = jnp.sum(jnp.log1p(carried), axis=1, keepdims=True)
    if groups * LANES < grown.shape[1]:
        total = total + jnp.sum(jnp.log1p(grown[:, groups * LANES :]), axis=1, keepdims=True)
    return total


def edges(left, rights, positive=False, losses=False):
    right = jnp.concatenate(rights, axis=0)
    product = lax.dot_general(left, right, ROW_COL, preferred_element_type=F32)
    grown = jnp.exp2(product * (LOGIT_SCALE * LOG2E) + LOGIT_BIAS * LOG2E)
    whole = 1.0 + grown
    weights = grown * pltpu.reciprocal(whole, approx=True)
    if positive:
        r = lax.broadcasted_iota(jnp.int32, product.shape, 0)
        c = lax.broadcasted_iota(jnp.int32, product.shape, 1)
        weights = jnp.where(r == c, weights - 1.0, weights)
    share = lax.dot_general(weights.astype(BF16), right, PLAIN, preferred_element_type=F32)
    if not losses:
        return share
    loss = soft_sum(grown, whole)
    if positive:
        logits = LOGIT_SCALE * product + LOGIT_BIAS
        loss = loss - jnp.sum(jnp.where(r == c, logits, 0.0), axis=1, keepdims=True)
    return share, loss


def halves(ref):
    rows = ref.shape[0] // 2
    return ref[pl.ds(0, rows), :], ref[pl.ds(rows, rows), :]


def in_parts(row):
    high = row.astype(BF16).astype(F32)
    middle = (row - high).astype(BF16).astype(F32)
    r = lax.broadcasted_iota(jnp.int32, (PACK, row.shape[1]), 0)
    low = jnp.where(r == 2, row - high - middle, 0.0)
    return jnp.where(r == 0, high, jnp.where(r == 1, middle, low)).astype(BF16)


def x_first(mate_text, x_near, z_near, z_far, share, loss, token):
    left = x_near[pl.ds(0, share.shape[0]), :]
    total, loss[...] = edges(left, [mate_text[...], z_near[...], z_far[...]], False, True)
    share[...] = (LOGIT_SCALE * total).astype(BF16)
    token[...] = jnp.zeros(token.shape, F32)


def x_second(mate_text, x_near, z_near, z_far, lost, _, share, token):
    rows = share.shape[0] - PACK
    left = x_near[pl.ds(x_near.shape[0] - rows, rows), :]
    total, loss = edges(left, [mate_text[...], z_near[...], z_far[...]], False, True)
    share[pl.ds(0, rows), :] = (LOGIT_SCALE * total).astype(BF16)
    share[pl.ds(rows, PACK), :] = jnp.zeros((PACK, share.shape[1]), BF16)
    row = as_row(jnp.concatenate([lost[...], loss], axis=0))
    share[pl.ds(rows, PACK), pl.ds(0, row.shape[1])] = in_parts(row)
    token[...] = jnp.zeros(token.shape, F32)


def mid_body(own, z_near, *rest):
    mates, (out, token) = rest[:-2], rest[-2:]
    out[...] = edges(z_near[...], [halves(own)[0]] + [mate[...] for mate in mates])
    token[...] = jnp.zeros(token.shape, F32)


def z_body(start, x_near, x_far, z_near, begun, _, share, token):
    part = pl.ds(start, share.shape[0])
    total = edges(z_near[part, :], [x_near[...], x_far[...]])
    share[...] = (LOGIT_SCALE * (begun[part, :] + total)).astype(BF16)
    token[...] = jnp.zeros(token.shape, F32)


def own_body(own, mate_text, x_far, z_near, z_far, _, *rest):
    mates, (i_out, t_out, loss_out) = rest[:-3], rest[-3:]
    image, text = halves(own)
    mate_text, mates = mate_text[...], [mate[...] for mate in mates]
    total, loss = edges(image, [text, mate_text, z_near[...], z_far[...]], True, True)
    i_out[...] = LOGIT_SCALE * total
    loss_out[...] = as_row(loss)
    t_out[...] = LOGIT_SCALE * edges(text, [image, *mates, x_far[...]], True)


def raw_gradient(raw, gradient):
    unit, inverse = normalize_rows(raw)
    return inverse * (gradient - unit * jnp.sum(unit * gradient, axis=1, keepdims=True))


def finish(start, raw, total, back, out, held, sems):
    pieces = sems.shape[0]
    rows = held.shape[0] // pieces
    copies = []
    for n in range(pieces):
        part, at = pl.ds(n * rows, rows), pl.ds(start + n * rows, rows)
        held[part, :] = raw_gradient(raw[at, :], total[at, :] + back[part, :].astype(F32))
        copies.append(pltpu.make_async_copy(held.at[part, :], out.at[at, :], sems.at[n]))
        copies[-1].start()
    return copies


def last_body(start, raw, total, back, *rest):
    token, out, held, sems = rest[-4:]
    token[...] = jnp.zeros(token.shape, F32)
    for copy in finish(start, raw, total, back, out, held, sems):
        copy.wait()


def final_body(start, raw, total, back, *rest):
    out, held, sems = rest[-3:]
    for copy in finish(start, raw, total, back, out, held, sems):
        copy.wait()


def loss_body(start, raw, total, back, i_loss, *rest):
    loss_out, token, out, held, sems, held_loss, loss_sem = rest[-7:]
    token[...] = jnp.zeros(token.shape, F32)
    rows = raw.shape[0]
    parts = back[pl.ds(rows - start, PACK), :].astype(F32)[:, :rows]
    loss = (i_loss[...] + jnp.sum(parts, axis=0, keepdims=True)) * (1.0 / rows)
    held_loss[...] = loss.reshape(held_loss.shape)
    copies = [pltpu.make_async_copy(held_loss, loss_out, loss_sem)]
    copies[0].start()
    for copy in copies + finish(start, raw, total, back, out, held, sems):
        copy.wait()


def last(start, count, raw, total, back, token, before=(), i_loss=()):
    args = (raw, total, back, *i_loss, token, *before)
    shapes, far_outs = [TOKEN, (raw.shape, F32)], (1,)
    scratch = [pltpu.VMEM((count, raw.shape[1]), F32), pltpu.SemaphoreType.DMA((count // 32,))]
    if i_loss:
        line = (raw.shape[0],)
        shapes, far_outs = [(line, F32)] + shapes, (0, 2)
        scratch += [pltpu.VMEM(line, F32), pltpu.SemaphoreType.DMA]
    body = loss_body if i_loss else last_body
    if before and not i_loss:
        body, shapes, far_outs = final_body, shapes[1:], (0,)
    return call(
        partial(body, start),
        shapes,
        args,
        far_args=(len(args) - 1,) if before else (),
        far_outs=far_outs,
        scratch=scratch,
        aliases={len(args) - 1: len(shapes) - 1} if before else None,
    )


def shards(image, text):
    rows, depth = image.shape
    block, pair = (rows, depth), (2 * rows, depth)
    first, second = FIRST, rows - FIRST
    z_near, x_near = swap(text, "z_lo"), swap(image, "x_hi")
    piece = ((rows // PIECES, depth), BF16)
    own, image, text, own_text, *own_image = call(
        own_norm, [(pair, BF16)] + [(block, BF16)] * 3 + [piece] * PIECES, (image, text)
    )
    mate_image = [swap(piece, "core") for piece in own_image]
    mate_text = swap(own_text, "core")
    (z_near,) = call(norm_body, [(block, BF16)], (z_near,))
    z_far = swap(z_near, "core")
    begun, token = call(mid_body, [(block, F32), TOKEN], (own, z_near, *mate_image))
    (x_near,) = call(norm_after, [(block, BF16)], (x_near, token), flops=4 * 10**9)
    x_far = swap(x_near, "core")
    share, x_loss, token = call(
        x_first, [((first, depth), BF16), ((first, 1), F32), TOKEN], (mate_text, x_near, z_near, z_far)
    )
    x_1 = swap(share, "x_hi")
    share, token = call(
        partial(z_body, 0),
        [((first, depth), BF16), TOKEN],
        (x_near, x_far, z_near, begun, token),
    )
    z_1 = swap(share, "z_lo")
    share, token = call(
        x_second,
        [((second + PACK, depth), BF16), TOKEN],
        (mate_text, x_near, z_near, z_far, x_loss, token),
    )
    x_2 = swap(share, "x_hi")
    share, token = call(
        partial(z_body, first),
        [((second, depth), BF16), TOKEN],
        (x_near, x_far, z_near, begun, token),
    )
    z_2 = swap(share, "z_lo")
    i_total, t_total, i_loss = call(
        own_body,
        [(block, F32), (block, F32), ((1, rows), F32)],
        (own, mate_text, x_far, z_near, z_far, token, *mate_image),
    )
    token, image_grad = last(0, first, image, i_total, x_1, token)
    token, text_grad = last(0, first, text, t_total, z_1, token)
    loss, token, image_grad = last(
        first, second, image, i_total, x_2, token, (image_grad,), (i_loss,)
    )
    (text_grad,) = last(first, second, text, t_total, z_2, token, (text_grad,))
    return (loss, image_grad, text_grad)


def solution(mesh):
    n_row, n_col = mesh.devices.shape
    fine = Mesh(mesh.devices.reshape(n_row // 2, 2, 2, n_col // 4, 2), AXES)
    return jax.shard_map(
        shards,
        mesh=fine,
        in_specs=(P(AXES, None), P(AXES, None)),
        out_specs=(P(AXES), P(AXES, None), P(AXES, None)),
        check_vma=False,
    )
```

```python
import math
from functools import partial

import jax
import jax.numpy as jnp
from jax import lax
from jax.experimental import pallas as pl
from jax.experimental.pallas import tpu as pltpu
from jax.sharding import Mesh
from jax.sharding import PartitionSpec as P

LOGIT_SCALE = 8.0
LOGIT_BIAS = -4.0
EPSILON = 1e-06
LOG2E = math.log2(math.e)
LANES = 128
ROW_COL = (((1,), (1,)), ((), ()))
PLAIN = (((1,), (0,)), ((), ()))
SWAP = ((0, 1), (1, 0))
AXES = ("outer", "core", "x_hi", "z_hi", "z_lo")
F32, BF16 = jnp.float32, jnp.bfloat16
MIB = 1024 * 1024
TOKEN = ((8, LANES), F32)
FIRST = 192
PACK = 16
PIECES = 1


def swap(value, axis):
    return lax.ppermute(value, axis, SWAP)


def call(body, shapes, args, far_args=(), far_outs=(), scratch=(), aliases=None, flops=1):
    vmem, far = pl.BlockSpec(memory_space=pltpu.VMEM), pl.BlockSpec(memory_space=pl.ANY)
    return pl.pallas_call(
        body,
        out_shape=[jax.ShapeDtypeStruct(s, d) for s, d in shapes],
        in_specs=[far if n in far_args else vmem for n in range(len(args))],
        out_specs=[far if n in far_outs else vmem for n in range(len(shapes))],
        scratch_shapes=scratch,
        input_output_aliases=aliases or {},
        compiler_params=pltpu.CompilerParams(vmem_limit_bytes=32 * MIB),
        cost_estimate=pl.CostEstimate(flops=flops, bytes_accessed=1, transcendentals=0),
    )(*args)


def normalize_rows(raw_rows):
    widened = raw_rows.astype(F32)
    inverse = lax.rsqrt(jnp.sum(widened * widened, axis=1, keepdims=True) + EPSILON)
    return (widened * inverse, inverse)


def norm_body(*refs):
    pieces, out = refs[:-1], refs[-1]
    rows = pieces[0].shape[0]
    for n, piece in enumerate(pieces):
        out[pl.ds(n * rows, rows), :] = normalize_rows(piece[...])[0].astype(BF16)


def norm_after(raw, _, out):
    norm_body(raw, out)


def own_norm(image, text, out, image_held, text_held, text_unit, *pieces):
    norm_body(image, text, out)
    text_unit[...] = halves(out)[1]
    rows = pieces[0].shape[0]
    for n, piece in enumerate(pieces):
        piece[...] = out[pl.ds(n * rows, rows), :]
    image_held[...] = image[...]
    text_held[...] = text[...]


def as_row(column):
    rows = column.shape[0]
    r = lax.broadcasted_iota(jnp.int32, (rows, rows), 0)
    c = lax.broadcasted_iota(jnp.int32, (rows, rows), 1)
    return jnp.sum(jnp.where(r == c, column, 0.0), axis=0, keepdims=True)


def soft_sum(grown, whole):
    total, groups = 0.0, grown.shape[1] // LANES
    carried = grown[:, :LANES]
    for n in range(1, groups):
        part = slice(n * LANES, (n + 1) * LANES)
        carried = carried * whole[:, part] + grown[:, part]
    total = jnp.sum(jnp.log1p(carried), axis=1, keepdims=True)
    if groups * LANES < grown.shape[1]:
        total = total + jnp.sum(jnp.log1p(grown[:, groups * LANES :]), axis=1, keepdims=True)
    return total


def edges(left, rights, positive=False, losses=False):
    right = jnp.concatenate(rights, axis=0)
    product = lax.dot_general(left, right, ROW_COL, preferred_element_type=F32)
    grown = jnp.exp2(product * (LOGIT_SCALE * LOG2E) + LOGIT_BIAS * LOG2E)
    whole = 1.0 + grown
    weights = grown * pltpu.reciprocal(whole, approx=True)
    if positive:
        r = lax.broadcasted_iota(jnp.int32, product.shape, 0)
        c = lax.broadcasted_iota(jnp.int32, product.shape, 1)
        weights = jnp.where(r == c, weights - 1.0, weights)
    share = lax.dot_general(weights.astype(BF16), right, PLAIN, preferred_element_type=F32)
    if not losses:
        return share
    loss = soft_sum(grown, whole)
    if positive:
        logits = LOGIT_SCALE * product + LOGIT_BIAS
        loss = loss - jnp.sum(jnp.where(r == c, logits, 0.0), axis=1, keepdims=True)
    return share, loss


def halves(ref):
    rows = ref.shape[0] // 2
    return ref[pl.ds(0, rows), :], ref[pl.ds(rows, rows), :]


def in_parts(row):
    high = row.astype(BF16).astype(F32)
    middle = (row - high).astype(BF16).astype(F32)
    r = lax.broadcasted_iota(jnp.int32, (PACK, row.shape[1]), 0)
    low = jnp.where(r == 2, row - high - middle, 0.0)
    return jnp.where(r == 0, high, jnp.where(r == 1, middle, low)).astype(BF16)


def x_first(mate_text, x_near, z_near, z_far, _, share, loss, token):
    left = x_near[pl.ds(0, share.shape[0]), :]
    total, loss[...] = edges(left, [mate_text[...], z_near[...], z_far[...]], False, True)
    share[...] = (LOGIT_SCALE * total).astype(BF16)
    token[...] = jnp.zeros(token.shape, F32)


def x_second(mate_text, x_near, z_near, z_far, lost, _, share, token):
    rows = share.shape[0] - PACK
    left = x_near[pl.ds(x_near.shape[0] - rows, rows), :]
    total, loss = edges(left, [mate_text[...], z_near[...], z_far[...]], False, True)
    share[pl.ds(0, rows), :] = (LOGIT_SCALE * total).astype(BF16)
    share[pl.ds(rows, PACK), :] = jnp.zeros((PACK, share.shape[1]), BF16)
    row = as_row(jnp.concatenate([lost[...], loss], axis=0))
    share[pl.ds(rows, PACK), pl.ds(0, row.shape[1])] = in_parts(row)
    token[...] = jnp.zeros(token.shape, F32)


def z_body(start, own, x_near, x_far, z_near, *rest):
    mates, (_, share, token) = rest[:-3], rest[-3:]
    part = pl.ds(start, share.shape[0])
    images = [halves(own)[0], *[mate[...] for mate in mates], x_near[...], x_far[...]]
    share[...] = (LOGIT_SCALE * edges(z_near[part, :], images)).astype(BF16)
    token[...] = jnp.zeros(token.shape, F32)


def own_body(own, mate_text, x_far, z_near, z_far, _, *rest):
    mates, (i_out, t_out, loss_out) = rest[:-3], rest[-3:]
    image, text = halves(own)
    mate_text, mates = mate_text[...], [mate[...] for mate in mates]
    total, loss = edges(image, [text, mate_text, z_near[...], z_far[...]], True, True)
    i_out[...] = LOGIT_SCALE * total
    loss_out[...] = as_row(loss)
    t_out[...] = LOGIT_SCALE * edges(text, [image, *mates, x_far[...]], True)


def raw_gradient(raw, gradient):
    unit, inverse = normalize_rows(raw)
    return inverse * (gradient - unit * jnp.sum(unit * gradient, axis=1, keepdims=True))


def finish(start, raw, total, back, out, held, sems):
    pieces = sems.shape[0]
    rows = held.shape[0] // pieces
    copies = []
    for n in range(pieces):
        part, at = pl.ds(n * rows, rows), pl.ds(start + n * rows, rows)
        held[part, :] = raw_gradient(raw[at, :], total[at, :] + back[part, :].astype(F32))
        copies.append(pltpu.make_async_copy(held.at[part, :], out.at[at, :], sems.at[n]))
        copies[-1].start()
    return copies


def last_body(start, raw, total, back, *rest):
    token, out, held, sems = rest[-4:]
    token[...] = jnp.zeros(token.shape, F32)
    for copy in finish(start, raw, total, back, out, held, sems):
        copy.wait()


def final_body(start, raw, total, back, *rest):
    out, held, sems = rest[-3:]
    for copy in finish(start, raw, total, back, out, held, sems):
        copy.wait()


def loss_body(start, raw, total, back, i_loss, *rest):
    loss_out, token, out, held, sems, held_loss, loss_sem = rest[-7:]
    token[...] = jnp.zeros(token.shape, F32)
    rows = raw.shape[0]
    parts = back[pl.ds(rows - start, PACK), :].astype(F32)[:, :rows]
    loss = (i_loss[...] + jnp.sum(parts, axis=0, keepdims=True)) * (1.0 / rows)
    held_loss[...] = loss.reshape(held_loss.shape)
    copies = [pltpu.make_async_copy(held_loss, loss_out, loss_sem)]
    copies[0].start()
    for copy in copies + finish(start, raw, total, back, out, held, sems):
        copy.wait()


def last(start, count, raw, total, back, token, before=(), i_loss=()):
    args = (raw, total, back, *i_loss, token, *before)
    shapes, far_outs = [TOKEN, (raw.shape, F32)], (1,)
    scratch = [pltpu.VMEM((count, raw.shape[1]), F32), pltpu.SemaphoreType.DMA((count // 32,))]
    if i_loss:
        line = (raw.shape[0],)
        shapes, far_outs = [(line, F32)] + shapes, (0, 2)
        scratch += [pltpu.VMEM(line, F32), pltpu.SemaphoreType.DMA]
    body = loss_body if i_loss else last_body
    if before and not i_loss:
        body, shapes, far_outs = final_body, shapes[1:], (0,)
    return call(
        partial(body, start),
        shapes,
        args,
        far_args=(len(args) - 1,) if before else (),
        far_outs=far_outs,
        scratch=scratch,
        aliases={len(args) - 1: len(shapes) - 1} if before else None,
    )


def shards(image, text):
    rows, depth = image.shape
    block, pair = (rows, depth), (2 * rows, depth)
    first, second = FIRST, rows - FIRST
    x_near, z_near = swap(image, "x_hi"), swap(text, "z_lo")
    piece = ((rows // PIECES, depth), BF16)
    own, image, text, own_text, *own_image = call(
        own_norm, [(pair, BF16)] + [(block, BF16)] * 3 + [piece] * PIECES, (image, text)
    )
    mate_image = [swap(piece, "core") for piece in own_image]
    mate_text = swap(own_text, "core")
    (x_near,) = call(norm_body, [(block, BF16)], (x_near,))
    x_far = swap(x_near, "core")
    (z_near,) = call(norm_body, [(block, BF16)], (z_near,), flops=4 * 10**9)
    z_far = swap(z_near, "core")
    share, token = call(
        partial(z_body, 0),
        [((first, depth), BF16), TOKEN],
        (own, x_near, x_far, z_near, *mate_image, z_near),
    )
    z_1 = swap(share, "z_lo")
    share, x_loss, token = call(
        x_first,
        [((first, depth), BF16), ((first, 1), F32), TOKEN],
        (mate_text, x_near, z_near, z_far, token),
    )
    x_1 = swap(share, "x_hi")
    share, token = call(
        x_second,
        [((second + PACK, depth), BF16), TOKEN],
        (mate_text, x_near, z_near, z_far, x_loss, token),
    )
    x_2 = swap(share, "x_hi")
    share, token = call(
        partial(z_body, first),
        [((second, depth), BF16), TOKEN],
        (own, x_near, x_far, z_near, *mate_image, token),
    )
    z_2 = swap(share, "z_lo")
    i_total, t_total, i_loss = call(
        own_body,
        [(block, F32), (block, F32), ((1, rows), F32)],
        (own, mate_text, x_far, z_near, z_far, token, *mate_image),
    )
    token, image_grad = last(0, first, image, i_total, x_1, token)
    token, text_grad = last(0, first, text, t_total, z_1, token)
    loss, token, image_grad = last(
        first, second, image, i_total, x_2, token, (image_grad,), (i_loss,)
    )
    (text_grad,) = last(first, second, text, t_total, z_2, token, (text_grad,))
    return (loss, image_grad, text_grad)


def solution(mesh):
    n_row, n_col = mesh.devices.shape
    fine = Mesh(mesh.devices.reshape(n_row // 2, 2, 2, n_col // 4, 2), AXES)
    return jax.shard_map(
        shards,
        mesh=fine,
        in_specs=(P(AXES, None), P(AXES, None)),
        out_specs=(P(AXES), P(AXES, None), P(AXES, None)),
        check_vma=False,
    )
```

```python
import math
from functools import partial

import jax
import jax.numpy as jnp
from jax import lax
from jax.experimental import pallas as pl
from jax.experimental.pallas import tpu as pltpu
from jax.sharding import Mesh
from jax.sharding import PartitionSpec as P

LOGIT_SCALE = 8.0
LOGIT_BIAS = -4.0
EPSILON = 1e-06
LOG2E = math.log2(math.e)
LANES = 128
ROW_COL = (((1,), (1,)), ((), ()))
PLAIN = (((1,), (0,)), ((), ()))
SWAP = ((0, 1), (1, 0))
AXES = ("outer", "core", "x_hi", "z_hi", "z_lo")
F32, BF16 = jnp.float32, jnp.bfloat16
MIB = 1024 * 1024
TOKEN = ((8, LANES), F32)
FIRST = 192
PACK = 16
PIECES = 1


def swap(value, axis):
    return lax.ppermute(value, axis, SWAP)


def call(body, shapes, args, far_args=(), far_outs=(), scratch=(), aliases=None, flops=1):
    vmem, far = pl.BlockSpec(memory_space=pltpu.VMEM), pl.BlockSpec(memory_space=pl.ANY)
    return pl.pallas_call(
        body,
        out_shape=[jax.ShapeDtypeStruct(s, d) for s, d in shapes],
        in_specs=[far if n in far_args else vmem for n in range(len(args))],
        out_specs=[far if n in far_outs else vmem for n in range(len(shapes))],
        scratch_shapes=scratch,
        input_output_aliases=aliases or {},
        compiler_params=pltpu.CompilerParams(vmem_limit_bytes=32 * MIB),
        cost_estimate=pl.CostEstimate(flops=flops, bytes_accessed=1, transcendentals=0),
    )(*args)


def normalize_rows(raw_rows):
    widened = raw_rows.astype(F32)
    inverse = lax.rsqrt(jnp.sum(widened * widened, axis=1, keepdims=True) + EPSILON)
    return (widened * inverse, inverse)


def norm_body(*refs):
    pieces, out = refs[:-1], refs[-1]
    rows = pieces[0].shape[0]
    for n, piece in enumerate(pieces):
        out[pl.ds(n * rows, rows), :] = normalize_rows(piece[...])[0].astype(BF16)


def norm_after(raw, _, out):
    norm_body(raw, out)


def own_norm(image, text, out, image_held, text_held, text_unit, *pieces):
    norm_body(image, text, out)
    text_unit[...] = halves(out)[1]
    rows = pieces[0].shape[0]
    for n, piece in enumerate(pieces):
        piece[...] = out[pl.ds(n * rows, rows), :]
    image_held[...] = image[...]
    text_held[...] = text[...]


def as_row(column):
    rows = column.shape[0]
    r = lax.broadcasted_iota(jnp.int32, (rows, rows), 0)
    c = lax.broadcasted_iota(jnp.int32, (rows, rows), 1)
    return jnp.sum(jnp.where(r == c, column, 0.0), axis=0, keepdims=True)


def soft_sum(grown, whole):
    total, groups = 0.0, grown.shape[1] // LANES
    carried = grown[:, :LANES]
    for n in range(1, groups):
        part = slice(n * LANES, (n + 1) * LANES)
        carried = carried * whole[:, part] + grown[:, part]
    total = jnp.sum(jnp.log1p(carried), axis=1, keepdims=True)
    if groups * LANES < grown.shape[1]:
        total = total + jnp.sum(jnp.log1p(grown[:, groups * LANES :]), axis=1, keepdims=True)
    return total


def edges(left, rights, positive=False, losses=False):
    right = jnp.concatenate(rights, axis=0)
    product = lax.dot_general(left, right, ROW_COL, preferred_element_type=F32)
    grown = jnp.exp2(product * (LOGIT_SCALE * LOG2E) + LOGIT_BIAS * LOG2E)
    whole = 1.0 + grown
    weights = grown * pltpu.reciprocal(whole, approx=True)
    if positive:
        r = lax.broadcasted_iota(jnp.int32, product.shape, 0)
        c = lax.broadcasted_iota(jnp.int32, product.shape, 1)
        weights = jnp.where(r == c, weights - 1.0, weights)
    share = lax.dot_general(weights.astype(BF16), right, PLAIN, preferred_element_type=F32)
    if not losses:
        return share
    loss = soft_sum(grown, whole)
    if positive:
        logits = LOGIT_SCALE * product + LOGIT_BIAS
        loss = loss - jnp.sum(jnp.where(r == c, logits, 0.0), axis=1, keepdims=True)
    return share, loss


def halves(ref):
    rows = ref.shape[0] // 2
    return ref[pl.ds(0, rows), :], ref[pl.ds(rows, rows), :]


def in_parts(row):
    high = row.astype(BF16).astype(F32)
    middle = (row - high).astype(BF16).astype(F32)
    r = lax.broadcasted_iota(jnp.int32, (PACK, row.shape[1]), 0)
    low = jnp.where(r == 2, row - high - middle, 0.0)
    return jnp.where(r == 0, high, jnp.where(r == 1, middle, low)).astype(BF16)


def x_first(mate_text, x_near, z_near, z_far, _, share, loss, token):
    left = x_near[pl.ds(0, share.shape[0]), :]
    total, loss[...] = edges(left, [mate_text[...], z_near[...], z_far[...]], False, True)
    share[...] = (LOGIT_SCALE * total).astype(BF16)
    token[...] = jnp.zeros(token.shape, F32)


def x_second(mate_text, x_near, z_near, z_far, lost, _, share, token):
    rows = share.shape[0] - PACK
    left = x_near[pl.ds(x_near.shape[0] - rows, rows), :]
    total, loss = edges(left, [mate_text[...], z_near[...], z_far[...]], False, True)
    share[pl.ds(0, rows), :] = (LOGIT_SCALE * total).astype(BF16)
    share[pl.ds(rows, PACK), :] = jnp.zeros((PACK, share.shape[1]), BF16)
    row = as_row(jnp.concatenate([lost[...], loss], axis=0))
    share[pl.ds(rows, PACK), pl.ds(0, row.shape[1])] = in_parts(row)
    token[...] = jnp.zeros(token.shape, F32)


def z_body(start, own, x_near, x_far, z_near, *rest):
    mates, (_, share, token) = rest[:-3], rest[-3:]
    part = pl.ds(start, share.shape[0])
    images = [halves(own)[0], *[mate[...] for mate in mates], x_near[...], x_far[...]]
    share[...] = (LOGIT_SCALE * edges(z_near[part, :], images)).astype(BF16)
    token[...] = jnp.zeros(token.shape, F32)


def pair_body(own, i_out, t_out, loss_out, token):
    image, text = halves(own)
    i_out[...], loss = edges(image, [text], True, True)
    loss_out[...] = as_row(loss)
    t_out[...] = edges(text, [image], True)
    token[...] = jnp.zeros(token.shape, F32)


def own_body(own, mate_text, x_far, z_near, z_far, _, i_in, t_in, loss_in, *rest):
    mates, (i_out, t_out, loss_out) = rest[:-3], rest[-3:]
    image, text = halves(own)
    mate_text, mates = mate_text[...], [mate[...] for mate in mates]
    total, loss = edges(image, [mate_text, z_near[...], z_far[...]], False, True)
    i_out[...] = LOGIT_SCALE * (i_in[...] + total)
    loss_out[...] = loss_in[...] + as_row(loss)
    t_out[...] = LOGIT_SCALE * (t_in[...] + edges(text, [*mates, x_far[...]]))


def raw_gradient(raw, gradient):
    unit, inverse = normalize_rows(raw)
    return inverse * (gradient - unit * jnp.sum(unit * gradient, axis=1, keepdims=True))


def finish(start, raw, total, back, out, held, sems):
    pieces = sems.shape[0]
    rows = held.shape[0] // pieces
    copies = []
    for n in range(pieces):
        part, at = pl.ds(n * rows, rows), pl.ds(start + n * rows, rows)
        held[part, :] = raw_gradient(raw[at, :], total[at, :] + back[part, :].astype(F32))
        copies.append(pltpu.make_async_copy(held.at[part, :], out.at[at, :], sems.at[n]))
        copies[-1].start()
    return copies


def last_body(start, raw, total, back, *rest):
    token, out, held, sems = rest[-4:]
    token[...] = jnp.zeros(token.shape, F32)
    for copy in finish(start, raw, total, back, out, held, sems):
        copy.wait()


def final_body(start, raw, total, back, *rest):
    out, held, sems = rest[-3:]
    for copy in finish(start, raw, total, back, out, held, sems):
        copy.wait()


def loss_body(start, raw, total, back, i_loss, *rest):
    loss_out, token, out, held, sems, held_loss, loss_sem = rest[-7:]
    token[...] = jnp.zeros(token.shape, F32)
    rows = raw.shape[0]
    parts = back[pl.ds(rows - start, PACK), :].astype(F32)[:, :rows]
    loss = (i_loss[...] + jnp.sum(parts, axis=0, keepdims=True)) * (1.0 / rows)
    held_loss[...] = loss.reshape(held_loss.shape)
    copies = [pltpu.make_async_copy(held_loss, loss_out, loss_sem)]
    copies[0].start()
    for copy in copies + finish(start, raw, total, back, out, held, sems):
        copy.wait()


def last(start, count, raw, total, back, token, before=(), i_loss=()):
    args = (raw, total, back, *i_loss, token, *before)
    shapes, far_outs = [TOKEN, (raw.shape, F32)], (1,)
    scratch = [pltpu.VMEM((count, raw.shape[1]), F32), pltpu.SemaphoreType.DMA((count // 32,))]
    if i_loss:
        line = (raw.shape[0],)
        shapes, far_outs = [(line, F32)] + shapes, (0, 2)
        scratch += [pltpu.VMEM(line, F32), pltpu.SemaphoreType.DMA]
    body = loss_body if i_loss else last_body
    if before and not i_loss:
        body, shapes, far_outs = final_body, shapes[1:], (0,)
    return call(
        partial(body, start),
        shapes,
        args,
        far_args=(len(args) - 1,) if before else (),
        far_outs=far_outs,
        scratch=scratch,
        aliases={len(args) - 1: len(shapes) - 1} if before else None,
    )


def shards(image, text):
    rows, depth = image.shape
    block, pair = (rows, depth), (2 * rows, depth)
    first, second = FIRST, rows - FIRST
    x_near, z_near = swap(image, "x_hi"), swap(text, "z_lo")
    piece = ((rows // PIECES, depth), BF16)
    own, image, text, own_text, *own_image = call(
        own_norm, [(pair, BF16)] + [(block, BF16)] * 3 + [piece] * PIECES, (image, text)
    )
    mate_image = [swap(piece, "core") for piece in own_image]
    mate_text = swap(own_text, "core")
    *own_parts, token = call(
        pair_body, [(block, F32), (block, F32), ((1, rows), F32), TOKEN], (own,)
    )
    (x_near,) = call(norm_after, [(block, BF16)], (x_near, token))
    x_far = swap(x_near, "core")
    (z_near,) = call(norm_body, [(block, BF16)], (z_near,), flops=4 * 10**9)
    z_far = swap(z_near, "core")
    share, token = call(
        partial(z_body, 0),
        [((first, depth), BF16), TOKEN],
        (own, x_near, x_far, z_near, *mate_image, z_near),
    )
    z_1 = swap(share, "z_lo")
    share, x_loss, token = call(
        x_first,
        [((first, depth), BF16), ((first, 1), F32), TOKEN],
        (mate_text, x_near, z_near, z_far, token),
    )
    x_1 = swap(share, "x_hi")
    share, token = call(
        x_second,
        [((second + PACK, depth), BF16), TOKEN],
        (mate_text, x_near, z_near, z_far, x_loss, token),
    )
    x_2 = swap(share, "x_hi")
    share, token = call(
        partial(z_body, first),
        [((second, depth), BF16), TOKEN],
        (own, x_near, x_far, z_near, *mate_image, token),
    )
    z_2 = swap(share, "z_lo")
    i_total, t_total, i_loss = call(
        own_body,
        [(block, F32), (block, F32), ((1, rows), F32)],
        (own, mate_text, x_far, z_near, z_far, token, *own_parts, *mate_image),
    )
    token, image_grad = last(0, first, image, i_total, x_1, token)
    token, text_grad = last(0, first, text, t_total, z_1, token)
    loss, token, image_grad = last(
        first, second, image, i_total, x_2, token, (image_grad,), (i_loss,)
    )
    (text_grad,) = last(first, second, text, t_total, z_2, token, (text_grad,))
    return (loss, image_grad, text_grad)


def solution(mesh):
    n_row, n_col = mesh.devices.shape
    fine = Mesh(mesh.devices.reshape(n_row // 2, 2, 2, n_col // 4, 2), AXES)
    return jax.shard_map(
        shards,
        mesh=fine,
        in_specs=(P(AXES, None), P(AXES, None)),
        out_specs=(P(AXES), P(AXES, None), P(AXES, None)),
        check_vma=False,
    )
```

```python
import math
from functools import partial

import jax
import jax.numpy as jnp
from jax import lax
from jax.experimental import pallas as pl
from jax.experimental.pallas import tpu as pltpu
from jax.sharding import Mesh
from jax.sharding import PartitionSpec as P

LOGIT_SCALE = 8.0
LOGIT_BIAS = -4.0
EPSILON = 1e-06
LOG2E = math.log2(math.e)
LANES = 128
ROW_COL = (((1,), (1,)), ((), ()))
PLAIN = (((1,), (0,)), ((), ()))
SWAP = ((0, 1), (1, 0))
AXES = ("outer", "core", "x_hi", "z_hi", "z_lo")
F32, BF16 = jnp.float32, jnp.bfloat16
MIB = 1024 * 1024
TOKEN = ((8, LANES), F32)
FIRST = 224
PACK = 16
PIECES = 1


def swap(value, axis):
    return lax.ppermute(value, axis, SWAP)


def call(body, shapes, args, far_args=(), far_outs=(), scratch=(), aliases=None, flops=1):
    vmem, far = pl.BlockSpec(memory_space=pltpu.VMEM), pl.BlockSpec(memory_space=pl.ANY)
    return pl.pallas_call(
        body,
        out_shape=[jax.ShapeDtypeStruct(s, d) for s, d in shapes],
        in_specs=[far if n in far_args else vmem for n in range(len(args))],
        out_specs=[far if n in far_outs else vmem for n in range(len(shapes))],
        scratch_shapes=scratch,
        input_output_aliases=aliases or {},
        compiler_params=pltpu.CompilerParams(vmem_limit_bytes=32 * MIB),
        cost_estimate=pl.CostEstimate(flops=flops, bytes_accessed=1, transcendentals=0),
    )(*args)


def normalize_rows(raw_rows):
    widened = raw_rows.astype(F32)
    inverse = lax.rsqrt(jnp.sum(widened * widened, axis=1, keepdims=True) + EPSILON)
    return (widened * inverse, inverse)


def norm_body(*refs):
    pieces, out = refs[:-1], refs[-1]
    rows = pieces[0].shape[0]
    for n, piece in enumerate(pieces):
        out[pl.ds(n * rows, rows), :] = normalize_rows(piece[...])[0].astype(BF16)


def norm_after(raw, _, out):
    norm_body(raw, out)


def own_norm(image, text, out, image_held, text_held, text_unit, *pieces):
    norm_body(image, text, out)
    text_unit[...] = halves(out)[1]
    rows = pieces[0].shape[0]
    for n, piece in enumerate(pieces):
        piece[...] = out[pl.ds(n * rows, rows), :]
    image_held[...] = image[...]
    text_held[...] = text[...]


def as_row(column):
    rows = column.shape[0]
    r = lax.broadcasted_iota(jnp.int32, (rows, rows), 0)
    c = lax.broadcasted_iota(jnp.int32, (rows, rows), 1)
    return jnp.sum(jnp.where(r == c, column, 0.0), axis=0, keepdims=True)


def soft_sum(grown, whole):
    total, groups = 0.0, grown.shape[1] // LANES
    carried = grown[:, :LANES]
    for n in range(1, groups):
        part = slice(n * LANES, (n + 1) * LANES)
        carried = carried * whole[:, part] + grown[:, part]
    total = jnp.sum(jnp.log1p(carried), axis=1, keepdims=True)
    if groups * LANES < grown.shape[1]:
        total = total + jnp.sum(jnp.log1p(grown[:, groups * LANES :]), axis=1, keepdims=True)
    return total


def edges(left, rights, positive=False, losses=False):
    right = jnp.concatenate(rights, axis=0)
    product = lax.dot_general(left, right, ROW_COL, preferred_element_type=F32)
    grown = jnp.exp2(product * (LOGIT_SCALE * LOG2E) + LOGIT_BIAS * LOG2E)
    whole = 1.0 + grown
    weights = grown * pltpu.reciprocal(whole, approx=True)
    if positive:
        r = lax.broadcasted_iota(jnp.int32, product.shape, 0)
        c = lax.broadcasted_iota(jnp.int32, product.shape, 1)
        weights = jnp.where(r == c, weights - 1.0, weights)
    share = lax.dot_general(weights.astype(BF16), right, PLAIN, preferred_element_type=F32)
    if not losses:
        return share
    loss = soft_sum(grown, whole)
    if positive:
        logits = LOGIT_SCALE * product + LOGIT_BIAS
        loss = loss - jnp.sum(jnp.where(r == c, logits, 0.0), axis=1, keepdims=True)
    return share, loss


def halves(ref):
    rows = ref.shape[0] // 2
    return ref[pl.ds(0, rows), :], ref[pl.ds(rows, rows), :]


def in_parts(row):
    high = row.astype(BF16).astype(F32)
    middle = (row - high).astype(BF16).astype(F32)
    r = lax.broadcasted_iota(jnp.int32, (PACK, row.shape[1]), 0)
    low = jnp.where(r == 2, row - high - middle, 0.0)
    return jnp.where(r == 0, high, jnp.where(r == 1, middle, low)).astype(BF16)


def x_first(mate_text, x_near, z_near, z_far, _, share, loss, token):
    left = x_near[pl.ds(0, share.shape[0]), :]
    total, loss[...] = edges(left, [mate_text[...], z_near[...], z_far[...]], False, True)
    share[...] = (LOGIT_SCALE * total).astype(BF16)
    token[...] = jnp.zeros(token.shape, F32)


def x_second(mate_text, x_near, z_near, z_far, lost, _, share, token):
    rows = share.shape[0] - PACK
    left = x_near[pl.ds(x_near.shape[0] - rows, rows), :]
    total, loss = edges(left, [mate_text[...], z_near[...], z_far[...]], False, True)
    share[pl.ds(0, rows), :] = (LOGIT_SCALE * total).astype(BF16)
    share[pl.ds(rows, PACK), :] = jnp.zeros((PACK, share.shape[1]), BF16)
    row = as_row(jnp.concatenate([lost[...], loss], axis=0))
    share[pl.ds(rows, PACK), pl.ds(0, row.shape[1])] = in_parts(row)
    token[...] = jnp.zeros(token.shape, F32)


def z_body(start, own, x_near, x_far, z_near, *rest):
    mates, (_, share, token) = rest[:-3], rest[-3:]
    part = pl.ds(start, share.shape[0])
    images = [halves(own)[0], *[mate[...] for mate in mates], x_near[...], x_far[...]]
    share[...] = (LOGIT_SCALE * edges(z_near[part, :], images)).astype(BF16)
    token[...] = jnp.zeros(token.shape, F32)


def pair_body(own, i_out, t_out, loss_out, token):
    image, text = halves(own)
    i_out[...], loss = edges(image, [text], True, True)
    loss_out[...] = as_row(loss)
    t_out[...] = edges(text, [image], True)
    token[...] = jnp.zeros(token.shape, F32)


def own_body(own, mate_text, x_far, z_near, z_far, _, i_in, t_in, loss_in, *rest):
    mates, (i_out, t_out, loss_out) = rest[:-3], rest[-3:]
    image, text = halves(own)
    mate_text, mates = mate_text[...], [mate[...] for mate in mates]
    total, loss = edges(image, [mate_text, z_near[...], z_far[...]], False, True)
    i_out[...] = LOGIT_SCALE * (i_in[...] + total)
    loss_out[...] = loss_in[...] + as_row(loss)
    t_out[...] = LOGIT_SCALE * (t_in[...] + edges(text, [*mates, x_far[...]]))


def raw_gradient(raw, gradient):
    unit, inverse = normalize_rows(raw)
    return inverse * (gradient - unit * jnp.sum(unit * gradient, axis=1, keepdims=True))


def finish(start, raw, total, back, out, held, sems):
    pieces = sems.shape[0]
    rows = held.shape[0] // pieces
    copies = []
    for n in range(pieces):
        part, at = pl.ds(n * rows, rows), pl.ds(start + n * rows, rows)
        held[part, :] = raw_gradient(raw[at, :], total[at, :] + back[part, :].astype(F32))
        copies.append(pltpu.make_async_copy(held.at[part, :], out.at[at, :], sems.at[n]))
        copies[-1].start()
    return copies


def last_body(start, raw, total, back, *rest):
    token, out, held, sems = rest[-4:]
    token[...] = jnp.zeros(token.shape, F32)
    for copy in finish(start, raw, total, back, out, held, sems):
        copy.wait()


def final_body(start, raw, total, back, *rest):
    out, held, sems = rest[-3:]
    for copy in finish(start, raw, total, back, out, held, sems):
        copy.wait()


def loss_body(start, raw, total, back, i_loss, *rest):
    loss_out, token, out, held, sems, held_loss, loss_sem = rest[-7:]
    token[...] = jnp.zeros(token.shape, F32)
    rows = raw.shape[0]
    parts = back[pl.ds(rows - start, PACK), :].astype(F32)[:, :rows]
    loss = (i_loss[...] + jnp.sum(parts, axis=0, keepdims=True)) * (1.0 / rows)
    held_loss[...] = loss.reshape(held_loss.shape)
    copies = [pltpu.make_async_copy(held_loss, loss_out, loss_sem)]
    copies[0].start()
    for copy in copies + finish(start, raw, total, back, out, held, sems):
        copy.wait()


def last(start, count, raw, total, back, token, before=(), i_loss=()):
    args = (raw, total, back, *i_loss, token, *before)
    shapes, far_outs = [TOKEN, (raw.shape, F32)], (1,)
    scratch = [pltpu.VMEM((count, raw.shape[1]), F32), pltpu.SemaphoreType.DMA((count // 32,))]
    if i_loss:
        line = (raw.shape[0],)
        shapes, far_outs = [(line, F32)] + shapes, (0, 2)
        scratch += [pltpu.VMEM(line, F32), pltpu.SemaphoreType.DMA]
    body = loss_body if i_loss else last_body
    if before and not i_loss:
        body, shapes, far_outs = final_body, shapes[1:], (0,)
    return call(
        partial(body, start),
        shapes,
        args,
        far_args=(len(args) - 1,) if before else (),
        far_outs=far_outs,
        scratch=scratch,
        aliases={len(args) - 1: len(shapes) - 1} if before else None,
    )


def shards(image, text):
    rows, depth = image.shape
    block, pair = (rows, depth), (2 * rows, depth)
    first, second = FIRST, rows - FIRST
    x_near, z_near = swap(image, "x_hi"), swap(text, "z_lo")
    piece = ((rows // PIECES, depth), BF16)
    own, image, text, own_text, *own_image = call(
        own_norm, [(pair, BF16)] + [(block, BF16)] * 3 + [piece] * PIECES, (image, text)
    )
    mate_image = [swap(piece, "core") for piece in own_image]
    mate_text = swap(own_text, "core")
    *own_parts, token = call(
        pair_body, [(block, F32), (block, F32), ((1, rows), F32), TOKEN], (own,)
    )
    (x_near,) = call(norm_after, [(block, BF16)], (x_near, token))
    x_far = swap(x_near, "core")
    (z_near,) = call(norm_body, [(block, BF16)], (z_near,), flops=4 * 10**9)
    z_far = swap(z_near, "core")
    share, token = call(
        partial(z_body, 0),
        [((first, depth), BF16), TOKEN],
        (own, x_near, x_far, z_near, *mate_image, z_near),
    )
    z_1 = swap(share, "z_lo")
    share, x_loss, token = call(
        x_first,
        [((first, depth), BF16), ((first, 1), F32), TOKEN],
        (mate_text, x_near, z_near, z_far, token),
    )
    x_1 = swap(share, "x_hi")
    share, token = call(
        x_second,
        [((second + PACK, depth), BF16), TOKEN],
        (mate_text, x_near, z_near, z_far, x_loss, token),
    )
    x_2 = swap(share, "x_hi")
    share, token = call(
        partial(z_body, first),
        [((second, depth), BF16), TOKEN],
        (own, x_near, x_far, z_near, *mate_image, token),
    )
    z_2 = swap(share, "z_lo")
    i_total, t_total, i_loss = call(
        own_body,
        [(block, F32), (block, F32), ((1, rows), F32)],
        (own, mate_text, x_far, z_near, z_far, token, *own_parts, *mate_image),
    )
    token, image_grad = last(0, first, image, i_total, x_1, token)
    token, text_grad = last(0, first, text, t_total, z_1, token)
    loss, token, image_grad = last(
        first, second, image, i_total, x_2, token, (image_grad,), (i_loss,)
    )
    (text_grad,) = last(first, second, text, t_total, z_2, token, (text_grad,))
    return (loss, image_grad, text_grad)


def solution(mesh):
    n_row, n_col = mesh.devices.shape
    fine = Mesh(mesh.devices.reshape(n_row // 2, 2, 2, n_col // 4, 2), AXES)
    return jax.shard_map(
        shards,
        mesh=fine,
        in_specs=(P(AXES, None), P(AXES, None)),
        out_specs=(P(AXES), P(AXES, None), P(AXES, None)),
        check_vma=False,
    )
```
